32 devices in a mesh: row: 4 (over y, core), col: 8 (over z, x).
Axes of the slice: x: 2, y: 2, z: 4, core: 2. Of those that a mesh axis runs over, the one named last changes fastest.
Arguments:
- inputs: bfloat16 [32, 128, 512], P('row', 'col'), may hold values from -6 to 6
- cotangent: bfloat16 [32, 128, 512], P('row', 'col'), may hold values from -6 to 6
- first_weight: bfloat16 [512, 256], replicated, may hold values from -0.25 to 0.25
- grouped_weight: bfloat16 [3, 3, 8, 256], replicated, may hold values from -0.75 to 0.75
- third_weight: bfloat16 [256, 512], replicated, may hold values from -0.375 to 0.375
- scale_first: float32 [256], replicated, may hold values from 0.5 to 2
- shift_first: float32 [256], replicated, may hold values from -0.5 to 0.5
- scale_mid: float32 [256], replicated, may hold values from 0.5 to 2
- shift_mid: float32 [256], replicated, may hold values from -0.5 to 0.5
- scale_third: float32 [512], replicated, may hold values from 0.5 to 2
- shift_third: float32 [512], replicated, may hold values from -0.5 to 0.5
Outputs:
- grad_input: bfloat16 [32, 128, 512], P('row', 'col')
- grad_first: float32 [512, 256], replicated
- grad_grouped: float32 [3, 3, 8, 256], replicated
- grad_third: float32 [256, 512], replicated
The draws below stay inside these ranges and needn't reach their ends.
All inputs are finite; a program needn't handle non-finite values.
Results may differ from the reference program's by a relative error of at most 0.0073.
Values may be sent and summed in bfloat16 or wider, within the bound.
A program may use at most 64 MiB of HBM per device.

```python
import math
import jax
import jax.numpy as jnp
from jax import lax

CIN = 512
HID = 256
GW = 8
H = 32
W = 128


def level_of(key, dims, split, low, top_value):
    gain = 1.0
    for position, shards_of in split:
        heights = jax.random.uniform(jax.random.fold_in(jax.random.fold_in(key, 6), position), (shards_of,), jnp.float32, low / len(split), top_value / len(split))
        gain = gain * jnp.repeat(jnp.exp(heights), dims[position] // shards_of).reshape((-1,) + (1,) * (len(dims) - 1 - position))
    return gain


def centred(own_key, extent, scale, bound, shards=(), kind=jnp.bfloat16):
    drawn = scale * jax.random.normal(own_key, extent, jnp.float32)
    if shards:
        drawn = drawn * level_of(own_key, extent, shards, -0.22, 0.18)
    return jnp.clip(drawn, -bound, bound).astype(kind)


def setup_inputs(seed: int = 0) -> dict:
    keys = jax.random.split(jax.random.key(seed), 12)
    return {
        "inputs": centred(keys[0], (H, W, CIN), 1.0, 6.0, ((0, 4), (1, 8))),
        "cotangent": centred(keys[1], (H, W, CIN), 1.0, 6.0, ((0, 4), (1, 8))),
        "first_weight": centred(keys[2], (CIN, HID), CIN ** -0.5, 0.25),
        "grouped_weight": centred(keys[3], (3, 3, GW, HID), (9 * GW) ** -0.5, 0.75),
        "third_weight": centred(keys[4], (HID, CIN), HID ** -0.5, 0.375),
        "scale_first": jnp.clip(jnp.exp(jax.random.uniform(keys[5], (HID,), jnp.float32, math.log(0.5), math.log(2.0))), 0.5, 2.0),
        "shift_first": jnp.clip(jax.random.uniform(keys[6], (HID,), jnp.float32, -0.5, 0.5), -0.5, 0.5),
        "scale_mid": jnp.clip(jnp.exp(jax.random.uniform(keys[7], (HID,), jnp.float32, math.log(0.5), math.log(2.0))), 0.5, 2.0),
        "shift_mid": jnp.clip(jax.random.uniform(keys[8], (HID,), jnp.float32, -0.5, 0.5), -0.5, 0.5),
        "scale_third": jnp.clip(jnp.exp(jax.random.uniform(keys[9], (CIN,), jnp.float32, math.log(0.5), math.log(2.0))), 0.5, 2.0),
        "shift_third": jnp.clip(jax.random.uniform(keys[10], (CIN,), jnp.float32, -0.5, 0.5), -0.5, 0.5),
    }


def silu_slope(values):
    logistic = jax.nn.sigmoid(values)
    return logistic * (1.0 + values * (1.0 - logistic))

def grouped_conv(padded, kernel, group_count):
    return lax.conv_general_dilated(padded[None], kernel, (1, 1), 'VALID', dimension_numbers=('NHWC', 'HWIO', 'NHWC'), feature_group_count=group_count, preferred_element_type=jnp.float32)[0]

def flip_kernel(kernel):
    width = kernel.shape[2]
    group_count = kernel.shape[3] // width
    flipped = kernel[::-1, ::-1].reshape(3, 3, width, group_count, width)
    return jnp.transpose(flipped, (0, 1, 4, 3, 2)).reshape(3, 3, width, group_count * width)

def tap_grads(padded_act, err_mid, group_count):
    tile_rows, tile_cols, hidden_dim = err_mid.shape
    width = hidden_dim // group_count
    err_groups = err_mid.reshape(tile_rows * tile_cols, group_count, width).astype(jnp.float32)
    taps = []
    for row_off in range(3):
        for col_off in range(3):
            window = padded_act[row_off:row_off + tile_rows, col_off:col_off + tile_cols].reshape(tile_rows * tile_cols, group_count, width).astype(jnp.float32)
            tapped = jnp.einsum('ngi,ngo->igo', window, err_groups)
            taps.append(tapped.reshape(width, hidden_dim))
    return jnp.stack(taps).reshape(3, 3, width, hidden_dim)

def contract_rows(left, right):
    return lax.dot_general(left, right, (((0,), (0,)), ((), ())), preferred_element_type=jnp.float32)

def contract_cols(left, right):
    return lax.dot_general(left, right, (((1,), (1,)), ((), ())), preferred_element_type=jnp.float32)

def reference(inputs, cotangent, first_weight, grouped_weight, third_weight, scale_first, shift_first, scale_mid, shift_mid, scale_third, shift_third):
    img_rows, img_cols, in_chans = inputs.shape
    hidden_dim = first_weight.shape[1]
    group_count = hidden_dim // grouped_weight.shape[2]
    flat_input = inputs.reshape(img_rows * img_cols, in_chans)
    pre_first = (jnp.dot(flat_input, first_weight, preferred_element_type=jnp.float32) * scale_first + shift_first).reshape(img_rows, img_cols, hidden_dim)
    act_first = jax.nn.silu(pre_first).astype(jnp.bfloat16)
    padded_act = jnp.pad(act_first, ((1, 1), (1, 1), (0, 0)))
    pre_mid = grouped_conv(padded_act, grouped_weight, group_count) * scale_mid + shift_mid
    act_mid = jax.nn.silu(pre_mid).astype(jnp.bfloat16)
    flat_mid = act_mid.reshape(img_rows * img_cols, hidden_dim)
    pre_third = jnp.dot(flat_mid, third_weight, preferred_element_type=jnp.float32) * scale_third + shift_third + flat_input.astype(jnp.float32)
    back_third = cotangent.reshape(img_rows * img_cols, in_chans).astype(jnp.float32) * silu_slope(pre_third)
    err_third = (back_third * scale_third).astype(jnp.bfloat16)
    grad_third = contract_rows(flat_mid, err_third)
    back_mid = contract_cols(err_third, third_weight).reshape(img_rows, img_cols, hidden_dim)
    err_mid = (back_mid * silu_slope(pre_mid) * scale_mid).astype(jnp.bfloat16)
    grad_grouped = tap_grads(padded_act, err_mid, group_count)
    err_padded = jnp.pad(err_mid, ((1, 1), (1, 1), (0, 0)))
    back_first = grouped_conv(err_padded, flip_kernel(grouped_weight), group_count)
    err_first = (back_first * silu_slope(pre_first) * scale_first).astype(jnp.bfloat16).reshape(img_rows * img_cols, hidden_dim)
    grad_first = contract_rows(flat_input, err_first)
    grad_input = (back_third + contract_cols(err_first, first_weight)).astype(jnp.bfloat16).reshape(img_rows, img_cols, in_chans)
    norm_factor = 1.0 / math.sqrt(H * W)
    return (grad_input, grad_first * norm_factor, grad_grouped * norm_factor, grad_third * norm_factor)
```

```python
import functools
import math

import jax
import jax.numpy as jnp
from jax import lax
from jax.experimental import pallas as pl
from jax.experimental.pallas import tpu as pltpu
from jax.sharding import PartitionSpec as P

MESH = pl.DeviceIdType.MESH
F32 = jnp.float32
BF16 = jnp.bfloat16
DIRS = [(dr, dc) for dr in (-1, 0, 1) for dc in (-1, 0, 1) if (dr, dc) != (0, 0)]
SLOT = {d: s for s, d in enumerate(DIRS)}
MSG = 16


def mm(left, right, lhs_dim=1, rhs_dim=0):
    return lax.dot_general(
        left, right, (((lhs_dim,), (rhs_dim,)), ((), ())), preferred_element_type=F32
    )


def remote(src, dst, send, recv, target):
    copy = pltpu.make_async_remote_copy(
        src_ref=src, dst_ref=dst, send_sem=send, recv_sem=recv, device_id=target, device_id_type=MESH
    )
    copy.start()
    return copy


def placement(th, tw, row, rows, col, cols):
    base = th * tw
    at = {d: base + MSG * s for d, s in SLOT.items()}
    cells = (th + 2) * tw
    index = lax.broadcasted_iota(jnp.int32, (cells, 1), 0)
    r = index // tw - 1
    c = index % tw
    far = 1 << 16
    no_up = (row == 0).astype(jnp.int32) * far
    no_down = (row == rows - 1).astype(jnp.int32) * far
    no_left = (col == 0).astype(jnp.int32) * far
    no_right = (col == cols - 1).astype(jnp.int32) * far
    up, down = r < 0, r >= th
    lanes = lax.broadcasted_iota(jnp.int32, (cells, base + 8 * MSG), 1)
    result = []
    for shift in (-1, 0, 1):
        cc = c + shift
        src = jnp.where(
            up, at[(-1, 0)] + cc - no_up, jnp.where(down, at[(1, 0)] + cc - no_down, r * tw + cc)
        )
        if shift == -1:
            edge = jnp.where(
                up,
                at[(-1, -1)] + tw - 1 - no_up,
                jnp.where(down, at[(1, -1)] + tw - 1 - no_down, at[(0, -1)] + th + r),
            )
            src = jnp.where(cc < 0, edge - no_left, src)
        if shift == 1:
            edge = jnp.where(
                up, at[(-1, 1)] - no_up, jnp.where(down, at[(1, 1)] - no_down, at[(0, 1)] + r)
            )
            src = jnp.where(cc >= tw, edge - no_right, src)
        result.append(jnp.where(src == lanes, 1.0, 0.0).astype(BF16))
    return result


def kernel(
    rows,
    cols,
    th,
    tw,
    x_ref,
    cot_ref,
    w1_ref,
    gw_ref,
    w3_ref,
    s1_ref,
    b1_ref,
    s2_ref,
    b2_ref,
    s3_ref,
    b3_ref,
    gin_ref,
    g1_ref,
    gk_ref,
    g3_ref,
    cells1,
    cells2,
    side1,
    side2,
    place,
    dense,
    padded1,
    padded2,
    slope1,
    slope2,
    back3,
    kgrad,
    t_part,
    t_rs,
    t_z,
    t_full,
    f_part,
    f_rs,
    f_z,
    f_full,
    halo_send,
    halo_recv,
    rs_send,
    rs_recv,
    z_send,
    z_recv,
    ag_send,
    ag_recv,
):
    row, col = lax.axis_index("row"), lax.axis_index("col")
    x, z = col % 2, col // 2
    depth = cols // 2
    plane_n = rows * 2
    me = row * 2 + x
    n = th * tw
    hid = w1_ref.shape[1]
    width = gw_ref.shape[0] // 9

    halo_peers = [
        (lax.rem(row + dr + rows, rows), lax.rem(col + dc + cols, cols)) for dr, dc in DIRS
    ]
    plane_peers = []
    for dr in range(rows):
        for dx in range(2):
            if dr or dx:
                plane_peers.append((lax.rem(row + dr, rows), z * 2 + lax.rem(x + dx, 2)))
    z_peers = [(row, lax.rem(z + dz, depth) * 2 + x) for dz in range(1, depth)]

    barrier = pltpu.get_barrier_semaphore()
    everyone = halo_peers + plane_peers + z_peers
    for peer in everyone:
        pl.semaphore_signal(barrier, inc=1, device_id=peer, device_id_type=MESH)

    def exchange(which, cells, side):
        copies = []
        for (dr, dc), peer in zip(DIRS, halo_peers):
            src = side
            if dr == -1:
                src = cells.at[pl.ds(0, tw)]
            elif dr == 1:
                src = cells.at[pl.ds(n - tw, tw)]
            there = SLOT[(-dr, -dc)]
            copies.append(
                remote(
                    src,
                    cells.at[pl.ds(n + there * MSG, MSG)],
                    halo_send.at[which, there],
                    halo_recv.at[which, there],
                    peer,
                )
            )
        return copies

    def scatter(which, part, slots):
        piece = slots.shape[1]
        copies = []
        for k, peer in enumerate(plane_peers):
            theirs = peer[0] * 2 + peer[1] % 2
            copies.append(
                remote(
                    part.at[pl.ds(pl.multiple_of(theirs * piece, 16), piece)],
                    slots.at[k],
                    rs_send.at[which, k],
                    rs_recv.at[which, k],
                    peer,
                )
            )
        return copies

    def sum_plane(copies, part, slots, total):
        piece = slots.shape[1]
        for copy in copies:
            copy.wait_recv()
        value = part[pl.ds(pl.multiple_of(me * piece, 16), piece), :].astype(F32)
        for k in range(plane_n - 1):
            value = value + slots[k].astype(F32)
        total[z] = value.astype(BF16)

    def spread(which, total):
        return [
            remote(
                total.at[z], total.at[z], z_send.at[which, k], z_recv.at[which, k], peer
            )
            for k, peer in enumerate(z_peers)
        ]

    def sum_depth(copies, total, full):
        piece = total.shape[1]
        for copy in copies:
            copy.wait_recv()
        value = total[0].astype(F32)
        for k in range(1, depth):
            value = value + total[k].astype(F32)
        full[pl.ds(pl.multiple_of(me * piece, 16), piece), :] = value.astype(BF16)

    def gather(which, total, full):
        piece = total.shape[1]
        mine = full.at[pl.ds(pl.multiple_of(me * piece, 16), piece)]
        return [
            remote(mine, mine, ag_send.at[which, k], ag_recv.at[which, k], peer)
            for k, peer in enumerate(plane_peers)
        ]

    pick_row = lax.broadcasted_iota(jnp.int32, (MSG, n), 0)
    pick_cell = lax.broadcasted_iota(jnp.int32, (MSG, n), 1)
    target = jnp.where(pick_row < th, pick_row * tw, (pick_row - th) * tw + tw - 1)
    pick = jnp.where(target == pick_cell, 1.0, 0.0).astype(BF16)

    pre1 = mm(x_ref[...], w1_ref[...]) * s1_ref[...] + b1_ref[...]
    sig = jax.nn.sigmoid(pre1)
    act1 = (pre1 * sig).astype(BF16)
    cells1[0:n, :] = act1
    side1[...] = mm(pick, act1).astype(BF16)
    pl.semaphore_wait(barrier, len(everyone))
    halo1 = exchange(0, cells1, side1)

    slope1[...] = sig * (1.0 + pre1 * (1.0 - sig)) * s1_ref[...]
    for b, matrix in enumerate(placement(th, tw, row, rows, col, cols)):
        place[b] = matrix
    same = (
        lax.broadcasted_iota(jnp.int32, (hid, hid), 0) // width
        == lax.broadcasted_iota(jnp.int32, (hid, hid), 1) // width
    )
    keep = jnp.where(same, 1.0, 0.0)
    grouped = gw_ref[...].astype(F32)
    for tap in range(9):
        small = grouped[tap * width : (tap + 1) * width]
        tiled = jnp.broadcast_to(small[None], (hid // width, width, hid)).reshape(hid, hid)
        dense[tap] = (tiled * keep).astype(BF16)
    kgrad[...] = jnp.zeros_like(kgrad)

    for copy in halo1:
        copy.wait_recv()
    for b in range(3):
        padded1[b] = mm(place[b], cells1[...]).astype(BF16)

    total = None
    for a in range(3):
        for b in range(3):
            term = mm(padded1[b, a * tw : a * tw + n, :], dense[a * 3 + b])
            total = term if total is None else total + term
    pre2 = total * s2_ref[...] + b2_ref[...]
    sig = jax.nn.sigmoid(pre2)
    act2 = (pre2 * sig).astype(BF16)
    slope2[...] = sig * (1.0 + pre2 * (1.0 - sig)) * s2_ref[...]

    pre3 = mm(act2, w3_ref[...]) * s3_ref[...] + b3_ref[...] + x_ref[...].astype(F32)
    sig = jax.nn.sigmoid(pre3)
    back = cot_ref[...].astype(F32) * (sig * (1.0 + pre3 * (1.0 - sig)))
    back3[...] = back
    err3 = (back * s3_ref[...]).astype(BF16)

    err2 = (mm(err3, w3_ref[...], 1, 1) * slope2[...]).astype(BF16)
    cells2[0:n, :] = err2
    side2[...] = mm(pick, err2).astype(BF16)
    halo2 = exchange(1, cells2, side2)

    third = mm(act2, err3, 0, 0)
    for half in range(third.shape[1] // hid):
        t_part[half * hid : (half + 1) * hid, :] = third[:, half * hid : (half + 1) * hid].astype(
            BF16
        )
    t_scatter = scatter(0, t_part, t_rs)
    for a in range(3):
        for b in range(3):
            tap = a * 3 + b
            square = mm(padded1[b, a * tw : a * tw + n, :], cells2[0:n, :], 0, 0) * keep
            kgrad[tap * width : (tap + 1) * width, :] = jnp.sum(
                square.reshape(hid // width, width, hid), axis=0
            )
    f_piece = f_rs.shape[1]
    k_piece = kgrad.shape[0] // plane_n
    w_piece = f_piece - k_piece
    for p in range(plane_n):
        f_part[p * f_piece + w_piece : (p + 1) * f_piece, :] = kgrad[
            p * k_piece : (p + 1) * k_piece, :
        ].astype(BF16)

    for copy in halo2:
        copy.wait_recv()
    for b in range(3):
        padded2[b] = mm(place[b], cells2[...]).astype(BF16)
    total = None
    for a in range(3):
        for b in range(3):
            window = padded2[2 - b, (2 - a) * tw : (2 - a) * tw + n, :]
            term = mm(window, dense[a * 3 + b], 1, 1)
            total = term if total is None else total + term
    err1 = (total * slope1[...]).astype(BF16)
    first = mm(x_ref[...], err1, 0, 0)
    for p in range(plane_n):
        f_part[p * f_piece : p * f_piece + w_piece, :] = first[
            p * w_piece : (p + 1) * w_piece
        ].astype(BF16)
    f_scatter = scatter(1, f_part, f_rs)

    sum_plane(t_scatter, t_part, t_rs, t_z)
    t_spread = spread(0, t_z)
    gin_ref[...] = (back3[...] + mm(err1, w1_ref[...], 1, 1)).astype(BF16)

    sum_plane(f_scatter, f_part, f_rs, f_z)
    f_spread = spread(1, f_z)
    sum_depth(t_spread, t_z, t_full)
    t_gather = gather(0, t_z, t_full)
    sum_depth(f_spread, f_z, f_full)
    f_gather = gather(1, f_z, f_full)

    for copy in t_gather:
        copy.wait_recv()
    for half in range(g3_ref.shape[1] // hid):
        g3_ref[:, half * hid : (half + 1) * hid] = t_full[half * hid : (half + 1) * hid, :]
    for copy in f_gather:
        copy.wait_recv()
    for p in range(plane_n):
        g1_ref[p * w_piece : (p + 1) * w_piece, :] = f_full[
            p * f_piece : p * f_piece + w_piece, :
        ]
        gk_ref[p * k_piece : (p + 1) * k_piece, :] = f_full[
            p * f_piece + w_piece : (p + 1) * f_piece, :
        ]
    for copy in halo1 + halo2 + t_scatter + f_scatter + t_spread + f_spread + t_gather + f_gather:
        copy.wait_send()


def body(mesh_rows, mesh_cols, inputs, cotangent, w1, gw, w3, s1, b1, s2, b2, s3, b3):
    th, tw, cin = inputs.shape
    hid = w1.shape[1]
    n = th * tw
    width = gw.shape[2]
    plane_n = mesh_rows * 2
    depth = mesh_cols // 2
    w_piece = cin // plane_n
    k_piece = -(-9 * width // plane_n)
    k_piece = -(-k_piece // 16) * 16
    f_piece = w_piece + k_piece
    vmem = pl.BlockSpec(memory_space=pltpu.VMEM)
    out_shape = (
        jax.ShapeDtypeStruct((n, cin), BF16),
        jax.ShapeDtypeStruct((cin, hid), BF16),
        jax.ShapeDtypeStruct((k_piece * plane_n, hid), BF16),
        jax.ShapeDtypeStruct((hid, cin), BF16),
    )
    cells = n + 8 * MSG
    padded = (3, (th + 2) * tw, hid)
    dma = pltpu.SemaphoreType.DMA
    gin, g1, gk, g3 = pl.pallas_call(
        functools.partial(kernel, mesh_rows, mesh_cols, th, tw),
        out_shape=out_shape,
        in_specs=[vmem] * 11,
        out_specs=(vmem,) * 4,
        scratch_shapes=[
            pltpu.VMEM((cells, hid), BF16),
            pltpu.VMEM((cells, hid), BF16),
            pltpu.VMEM((MSG, hid), BF16),
            pltpu.VMEM((MSG, hid), BF16),
            pltpu.VMEM((3, (th + 2) * tw, cells), BF16),
            pltpu.VMEM((9, hid, hid), BF16),
            pltpu.VMEM(padded, BF16),
            pltpu.VMEM(padded, BF16),
            pltpu.VMEM((n, hid), F32),
            pltpu.VMEM((n, hid), F32),
            pltpu.VMEM((n, cin), F32),
            pltpu.VMEM((k_piece * plane_n, hid), F32),
            pltpu.VMEM((cin, hid), BF16),
            pltpu.VMEM((plane_n - 1, w_piece, hid), BF16),
            pltpu.VMEM((depth, w_piece, hid), BF16),
            pltpu.VMEM((cin, hid), BF16),
            pltpu.VMEM((plane_n * f_piece, hid), BF16),
            pltpu.VMEM((plane_n - 1, f_piece, hid), BF16),
            pltpu.VMEM((depth, f_piece, hid), BF16),
            pltpu.VMEM((plane_n * f_piece, hid), BF16),
            dma((2, 8)),
            dma((2, 8)),
            dma((2, plane_n - 1)),
            dma((2, plane_n - 1)),
            dma((2, depth - 1)),
            dma((2, depth - 1)),
            dma((2, plane_n - 1)),
            dma((2, plane_n - 1)),
        ],
        compiler_params=pltpu.CompilerParams(
            collective_id=0, has_side_effects=True, vmem_limit_bytes=40 << 20
        ),
    )(
        inputs.reshape(n, cin),
        cotangent.reshape(n, cin),
        w1,
        gw.reshape(9 * width, hid),
        w3,
        s1.reshape(1, -1),
        b1.reshape(1, -1),
        s2.reshape(1, -1),
        b2.reshape(1, -1),
        s3.reshape(1, -1),
        b3.reshape(1, -1),
    )
    norm = 1.0 / math.sqrt(n * mesh_rows * mesh_cols)
    return (
        gin.reshape(th, tw, cin),
        g1.astype(F32) * norm,
        (gk[: 9 * width].astype(F32) * norm).reshape(gw.shape),
        g3.astype(F32) * norm,
    )


def solution(mesh):
    tile = P("row", "col", None)
    return jax.shard_map(
        functools.partial(body, mesh.shape["row"], mesh.shape["col"]),
        mesh=mesh,
        in_specs=(tile, tile) + (P(),) * 9,
        out_specs=(tile, P(), P(), P()),
        check_vma=False,
    )
```

```python
import functools
import math

import jax
import jax.numpy as jnp
from jax import lax
from jax.experimental import pallas as pl
from jax.experimental.pallas import tpu as pltpu
from jax.sharding import PartitionSpec as P

MESH = pl.DeviceIdType.MESH
F32 = jnp.float32
BF16 = jnp.bfloat16
DIRS = [(dr, dc) for dr in (-1, 0, 1) for dc in (-1, 0, 1) if (dr, dc) != (0, 0)]
SLOT = {d: s for s, d in enumerate(DIRS)}
MSG = 16
PARTS = 2
LOAD_ORDER = (0, 2, 5, 6, 3, 7, 8, 4, 9, 10, 1)


def mm(left, right, lhs_dim=1, rhs_dim=0):
    return lax.dot_general(
        left, right, (((lhs_dim,), (rhs_dim,)), ((), ())), preferred_element_type=F32
    )


def remote(src, dst, send, recv, target):
    copy = pltpu.make_async_remote_copy(
        src_ref=src, dst_ref=dst, send_sem=send, recv_sem=recv, device_id=target, device_id_type=MESH
    )
    copy.start()
    return copy


def placement(th, tw, row, rows, col, cols):
    base = th * tw
    at = {d: base + MSG * s for d, s in SLOT.items()}
    cells = (th + 2) * tw
    index = lax.broadcasted_iota(jnp.int32, (cells, 1), 0)
    r = index // tw - 1
    c = index % tw
    far = 1 << 16
    no_up = (row == 0).astype(jnp.int32) * far
    no_down = (row == rows - 1).astype(jnp.int32) * far
    no_left = (col == 0).astype(jnp.int32) * far
    no_right = (col == cols - 1).astype(jnp.int32) * far
    up, down = r < 0, r >= th
    lanes = lax.broadcasted_iota(jnp.int32, (cells, base + 8 * MSG), 1)
    result = []
    for shift in (-1, 0, 1):
        cc = c + shift
        src = jnp.where(
            up, at[(-1, 0)] + cc - no_up, jnp.where(down, at[(1, 0)] + cc - no_down, r * tw + cc)
        )
        if shift == -1:
            edge = jnp.where(
                up,
                at[(-1, -1)] + tw - 1 - no_up,
                jnp.where(down, at[(1, -1)] + tw - 1 - no_down, at[(0, -1)] + th + r),
            )
            src = jnp.where(cc < 0, edge - no_left, src)
        if shift == 1:
            edge = jnp.where(
                up, at[(-1, 1)] - no_up, jnp.where(down, at[(1, 1)] - no_down, at[(0, 1)] + r)
            )
            src = jnp.where(cc >= tw, edge - no_right, src)
        result.append(jnp.where(src == lanes, 1.0, 0.0).astype(BF16))
    return result


def kernel(rows, cols, th, tw, chunks, norm, *refs):
    hbm, refs = refs[:11], refs[11:]
    outs = refs[:4]
    local, refs = refs[4:15], refs[15:]
    x_ref, cot_ref, w1_ref, gw_ref, w3_ref, s1_ref, b1_ref, s2_ref, b2_ref, s3_ref, b3_ref = local
    cells1, cells2, side1, side2, place, dense, padded1, padded2 = refs[:8]
    slope1, slope2, back3, kgrad, x_turned = refs[8:13]
    gin_ref, g1_ref, gk_ref, g3_ref = refs[13:17]
    refs = refs[4:]
    units = [refs[13 + 4 * u : 17 + 4 * u] for u in range(2 + chunks)]
    (load_sem, out_sem, halo_send, halo_recv, rs_send, rs_recv, z_send, z_recv, ag_send, ag_recv) = refs[
        13 + 4 * (2 + chunks) :
    ]
    loads = []
    for index in LOAD_ORDER:
        copy = pltpu.make_async_copy(hbm[index], local[index], load_sem.at[index])
        copy.start()
        loads.append(copy)
    row, col = lax.axis_index("row"), lax.axis_index("col")
    x, z = col % 2, col // 2
    depth = cols // 2
    plane_n = rows * 2
    me = row * 2 + x
    n = th * tw
    hid = w1_ref.shape[1]
    width = gw_ref.shape[0] // 9

    halo_peers = [
        (lax.rem(row + dr + rows, rows), lax.rem(col + dc + cols, cols)) for dr, dc in DIRS
    ]
    plane_peers = []
    for dr in range(rows):
        for dx in range(2):
            if dr or dx:
                plane_peers.append((lax.rem(row + dr, rows), z * 2 + lax.rem(x + dx, 2)))
    z_peers = [(row, lax.rem(z + dz, depth) * 2 + x) for dz in range(1, depth)]

    def exists(dr, dc):
        ok = None
        for step, spot, count in ((dr, row, rows), (dc, col, cols)):
            if step:
                inside = spot > 0 if step < 0 else spot < count - 1
                ok = inside if ok is None else jnp.logical_and(ok, inside)
        return ok

    for cells in (cells1, cells2):
        cells[n:, :] = jnp.zeros((8 * MSG, hid), BF16)

    barrier = pltpu.get_barrier_semaphore()
    for peer in plane_peers + z_peers:
        pl.semaphore_signal(barrier, inc=1, device_id=peer, device_id_type=MESH)
    for (dr, dc), peer in zip(DIRS, halo_peers):

        @pl.when(exists(dr, dc))
        def _(peer=peer):
            pl.semaphore_signal(barrier, inc=1, device_id=peer, device_id_type=MESH)

    near_rows = 1 + (row > 0).astype(jnp.int32) + (row < rows - 1).astype(jnp.int32)
    near_cols = 1 + (col > 0).astype(jnp.int32) + (col < cols - 1).astype(jnp.int32)
    greeted = near_rows * near_cols - 1 + len(plane_peers) + len(z_peers)

    def border(which, cells, side, d, arriving):
        dr, dc = d
        src = side
        if dr == -1:
            src = cells.at[pl.ds(0, tw)]
        elif dr == 1:
            src = cells.at[pl.ds(n - tw, tw)]
        slot = SLOT[d] if arriving else SLOT[(-dr, -dc)]
        return pltpu.make_async_remote_copy(
            src_ref=src,
            dst_ref=cells.at[pl.ds(n + slot * MSG, MSG)],
            send_sem=halo_send.at[which, slot],
            recv_sem=halo_recv.at[which, slot],
            device_id=halo_peers[SLOT[d]],
            device_id_type=MESH,
        )

    def exchange(which, cells, side):
        for d in DIRS:

            @pl.when(exists(*d))
            def _(d=d):
                border(which, cells, side, d, False).start()

    def arrive(which, cells, side):
        for d in DIRS:

            @pl.when(exists(*d))
            def _(d=d):
                border(which, cells, side, d, True).wait_recv()

    def depart(which, cells, side):
        for d in DIRS:

            @pl.when(exists(*d))
            def _(d=d):
                border(which, cells, side, d, False).wait_send()

    def scatter(which, part, slots):
        piece = slots.shape[1]
        copies = []
        for k, peer in enumerate(plane_peers):
            theirs = peer[0] * 2 + peer[1] % 2
            copies.append(
                remote(
                    part.at[pl.ds(pl.multiple_of(theirs * piece, 16), piece)],
                    slots.at[k],
                    rs_send.at[which, k],
                    rs_recv.at[which, k],
                    peer,
                )
            )
        return copies

    def sum_plane(copies, part, slots, total):
        piece = slots.shape[1]
        for copy in copies:
            copy.wait_recv()
        value = part[pl.ds(pl.multiple_of(me * piece, 16), piece), :].astype(F32)
        for k in range(plane_n - 1):
            value = value + slots[k].astype(F32)
        total[z] = value.astype(BF16)

    def spread(which, total):
        return [
            remote(
                total.at[z], total.at[z], z_send.at[which, k], z_recv.at[which, k], peer
            )
            for k, peer in enumerate(z_peers)
        ]

    def sum_depth(copies, total, full):
        piece = total.shape[1]
        for copy in copies:
            copy.wait_recv()
        value = total[0].astype(F32)
        for k in range(1, depth):
            value = value + total[k].astype(F32)
        full[pl.ds(pl.multiple_of(me * piece, 16), piece), :] = value.astype(BF16)

    def gather(which, total, full):
        piece = total.shape[1]
        mine = full.at[pl.ds(pl.multiple_of(me * piece, 16), piece)]
        return [
            remote(mine, mine, ag_send.at[which, k], ag_recv.at[which, k], peer)
            for k, peer in enumerate(plane_peers)
        ]

    pick_row = lax.broadcasted_iota(jnp.int32, (MSG, n), 0)
    pick_cell = lax.broadcasted_iota(jnp.int32, (MSG, n), 1)
    target = jnp.where(pick_row < th, pick_row * tw, (pick_row - th) * tw + tw - 1)
    pick = jnp.where(target == pick_cell, 1.0, 0.0).astype(BF16)

    for copy in loads[:4]:
        copy.wait()
    pre1 = mm(x_ref[...], w1_ref[...]) * s1_ref[...] + b1_ref[...]
    sig = jax.nn.sigmoid(pre1)
    act1 = (pre1 * sig).astype(BF16)
    cells1[0:n, :] = act1
    side1[...] = mm(pick, act1).astype(BF16)
    pl.semaphore_wait(barrier, greeted)
    exchange(0, cells1, side1)
    for copy in loads[4:]:
        copy.wait()

    slope1[...] = sig * (1.0 + pre1 * (1.0 - sig)) * s1_ref[...]
    for b, matrix in enumerate(placement(th, tw, row, rows, col, cols)):
        place[b] = matrix
    same = (
        lax.broadcasted_iota(jnp.int32, (hid, hid), 0) // width
        == lax.broadcasted_iota(jnp.int32, (hid, hid), 1) // width
    )
    keep = jnp.where(same, 1.0, 0.0)
    grouped = gw_ref[...].astype(F32)
    for tap in range(9):
        small = grouped[tap * width : (tap + 1) * width]
        tiled = jnp.broadcast_to(small[None], (hid // width, width, hid)).reshape(hid, hid)
        dense[tap] = (tiled * keep).astype(BF16)
    kgrad[...] = jnp.zeros_like(kgrad)

    x_turned[...] = x_ref[...].T

    arrive(0, cells1, side1)
    for b in range(3):
        padded1[b] = mm(place[b], cells1[...]).astype(BF16)

    total = None
    for a in range(3):
        for b in range(3):
            term = mm(padded1[b, a * tw : a * tw + n, :], dense[a * 3 + b])
            total = term if total is None else total + term
    pre2 = total * s2_ref[...] + b2_ref[...]
    sig = jax.nn.sigmoid(pre2)
    act2 = (pre2 * sig).astype(BF16)
    slope2[...] = sig * (1.0 + pre2 * (1.0 - sig)) * s2_ref[...]

    pre3 = mm(act2, w3_ref[...]) * s3_ref[...] + b3_ref[...] + x_ref[...].astype(F32)
    sig = jax.nn.sigmoid(pre3)
    back = cot_ref[...].astype(F32) * (sig * (1.0 + pre3 * (1.0 - sig)))
    back3[...] = back
    err3 = (back * s3_ref[...]).astype(BF16)

    err2 = (mm(err3, w3_ref[...], 1, 1) * slope2[...]).astype(BF16)
    cells2[0:n, :] = err2
    side2[...] = mm(pick, err2).astype(BF16)
    exchange(1, cells2, side2)

    started = []

    def unit(index, step, *extra):
        part, slots, total, full = units[index]
        if step == 0:
            copies = scatter(index, part, slots)
        elif step == 1:
            sum_plane(*extra, part, slots, total)
            copies = spread(index, total)
        else:
            sum_depth(*extra, total, full)
            copies = gather(index, total, full)
        started.extend(copies)
        return copies

    third = mm(act2, err3, 0, 0)
    for half in range(third.shape[1] // hid):
        units[0][0][half * hid : (half + 1) * hid, :] = third[
            :, half * hid : (half + 1) * hid
        ].astype(BF16)
    t_now = unit(0, 0)
    for a in range(3):
        for b in range(3):
            tap = a * 3 + b
            square = mm(padded1[b, a * tw : a * tw + n, :], cells2[0:n, :], 0, 0) * keep
            kgrad[tap * width : (tap + 1) * width, :] = jnp.sum(
                square.reshape(hid // width, width, hid), axis=0
            )
    units[1][0][...] = kgrad[...].astype(BF16)
    k_now = unit(1, 0)

    arrive(1, cells2, side2)
    for b in range(3):
        padded2[b] = mm(place[b], cells2[...]).astype(BF16)
    total = None
    for a in range(3):
        for b in range(3):
            window = padded2[2 - b, (2 - a) * tw : (2 - a) * tw + n, :]
            term = mm(window, dense[a * 3 + b], 1, 1)
            total = term if total is None else total + term
    err1 = (total * slope1[...]).astype(BF16)
    span = hid // chunks
    f_now = []
    for chunk in range(chunks):
        units[2 + chunk][0][...] = mm(
            x_turned[...], err1[:, chunk * span : (chunk + 1) * span]
        ).astype(BF16)
        f_now.append(unit(2 + chunk, 0))

    t_now = unit(0, 1, t_now)
    k_now = unit(1, 1, k_now)
    for chunk in range(chunks):
        f_now[chunk] = unit(2 + chunk, 1, f_now[chunk])
    t_now = unit(0, 2, t_now)
    k_now = unit(1, 2, k_now)
    for chunk in range(chunks):
        f_now[chunk] = unit(2 + chunk, 2, f_now[chunk])
    gin_ref[...] = (back3[...] + mm(err1, w1_ref[...], 1, 1)).astype(BF16)
    stores = []

    def store(src, dst):
        copy = pltpu.make_async_copy(src, dst, out_sem.at[len(stores)])
        copy.start()
        stores.append(copy)

    store(gin_ref, outs[0])
    for copy in t_now:
        copy.wait_recv()
    for half in range(g3_ref.shape[1] // hid):
        g3_ref[:, half * hid : (half + 1) * hid] = (
            units[0][3][half * hid : (half + 1) * hid, :].astype(F32) * norm
        )
    store(g3_ref, outs[3])
    for copy in k_now:
        copy.wait_recv()
    gk_ref[...] = units[1][3][...].astype(F32)[: gk_ref.shape[0]] * norm
    store(gk_ref, outs[2])
    for chunk in range(chunks):
        for copy in f_now[chunk]:
            copy.wait_recv()
        lanes = pl.ds(chunk * span, span)
        g1_ref[:, lanes] = units[2 + chunk][3][...].astype(F32) * norm
        store(g1_ref.at[:, lanes], outs[1].at[:, lanes])
    depart(0, cells1, side1)
    depart(1, cells2, side2)
    for copy in started:
        copy.wait_send()
    for copy in stores:
        copy.wait()


def finish(*refs):
    sources, targets, held, sems = refs[:4], refs[4:8], refs[8:12], refs[12]
    reads, writes = [], []
    for k, (src, dst, hold) in enumerate(zip(sources, targets, held)):
        parts = PARTS if src.shape[0] % (16 * PARTS) == 0 else 1
        size = src.shape[0] // parts
        for part in range(parts):
            span = pl.ds(part * size, size)
            reads.append(pltpu.make_async_copy(src.at[span], hold.at[span], sems.at[0, k, part]))
            writes.append(pltpu.make_async_copy(hold.at[span], dst.at[span], sems.at[1, k, part]))
    for copy in reads:
        copy.start()
    for read, write in zip(reads, writes):
        read.wait()
        write.start()
    for copy in writes:
        copy.wait()


def body(mesh_rows, mesh_cols, inputs, cotangent, w1, gw, w3, s1, b1, s2, b2, s3, b3):
    th, tw, cin = inputs.shape
    hid = w1.shape[1]
    n = th * tw
    width = gw.shape[2]
    plane_n = mesh_rows * 2
    depth = mesh_cols // 2
    chunks = 2
    w_piece = cin // plane_n
    k_piece = -(-9 * width // plane_n)
    k_piece = -(-k_piece // 16) * 16
    hbm = pl.BlockSpec(memory_space=pltpu.HBM)
    out_shape = (
        jax.ShapeDtypeStruct((n, cin), BF16),
        jax.ShapeDtypeStruct((cin, hid), F32),
        jax.ShapeDtypeStruct((9 * width, hid), F32),
        jax.ShapeDtypeStruct((hid, cin), F32),
    )
    norm = 1.0 / math.sqrt(n * mesh_rows * mesh_cols)
    operands = (
        inputs.reshape(n, cin),
        cotangent.reshape(n, cin),
        w1,
        gw.reshape(9 * width, hid),
        w3,
        s1.reshape(1, -1),
        b1.reshape(1, -1),
        s2.reshape(1, -1),
        b2.reshape(1, -1),
        s3.reshape(1, -1),
        b3.reshape(1, -1),
    )
    cells = n + 8 * MSG
    padded = (3, (th + 2) * tw, hid)
    dma = pltpu.SemaphoreType.DMA
    unit_shapes = [(w_piece, hid), (k_piece, hid)] + [(w_piece, hid // chunks)] * chunks
    unit_scratch = []
    for piece, wide in unit_shapes:
        for shape in (
            (plane_n * piece, wide),
            (plane_n - 1, piece, wide),
            (depth, piece, wide),
            (plane_n * piece, wide),
        ):
            unit_scratch.append(pltpu.VMEM(shape, BF16))
    count = 2 + chunks
    results = pl.pallas_call(
        functools.partial(kernel, mesh_rows, mesh_cols, th, tw, chunks, norm),
        out_shape=out_shape,
        in_specs=[hbm] * 11,
        out_specs=(hbm,) * 4,
        scratch_shapes=[pltpu.VMEM(a.shape, a.dtype) for a in operands]
        + [
            pltpu.VMEM((cells, hid), BF16),
            pltpu.VMEM((cells, hid), BF16),
            pltpu.VMEM((MSG, hid), BF16),
            pltpu.VMEM((MSG, hid), BF16),
            pltpu.VMEM((3, (th + 2) * tw, cells), BF16),
            pltpu.VMEM((9, hid, hid), BF16),
            pltpu.VMEM(padded, BF16),
            pltpu.VMEM(padded, BF16),
            pltpu.VMEM((n, hid), F32),
            pltpu.VMEM((n, hid), F32),
            pltpu.VMEM((n, cin), F32),
            pltpu.VMEM((k_piece * plane_n, hid), F32),
            pltpu.VMEM((cin, n), BF16),
        ]
        + [pltpu.VMEM(a.shape, a.dtype) for a in out_shape]
        + unit_scratch
        + [
            dma((11,)),
            dma((3 + chunks,)),
            dma((2, 8)),
            dma((2, 8)),
            dma((count, plane_n - 1)),
            dma((count, plane_n - 1)),
            dma((count, depth - 1)),
            dma((count, depth - 1)),
            dma((count, plane_n - 1)),
            dma((count, plane_n - 1)),
        ],
        compiler_params=pltpu.CompilerParams(
            collective_id=0, has_side_effects=True, vmem_limit_bytes=60 << 20
        ),
    )(*operands)
    gin, g1, gk, g3 = pl.pallas_call(
        finish,
        out_shape=out_shape,
        in_specs=[hbm] * 4,
        out_specs=(hbm,) * 4,
        scratch_shapes=[pltpu.VMEM(a.shape, a.dtype) for a in out_shape] + [dma((2, 4, PARTS))],
        compiler_params=pltpu.CompilerParams(vmem_limit_bytes=60 << 20),
    )(*results)
    return gin.reshape(th, tw, cin), g1, gk.reshape(gw.shape), g3


def solution(mesh):
    tile = P("row", "col", None)
    return jax.shard_map(
        functools.partial(body, mesh.shape["row"], mesh.shape["col"]),
        mesh=mesh,
        in_specs=(tile, tile) + (P(),) * 9,
        out_specs=(tile, P(), P(), P()),
        check_vma=False,
    )
```

```python
import functools
import math

import jax
import jax.numpy as jnp
from jax import lax
from jax.experimental import pallas as pl
from jax.experimental.pallas import tpu as pltpu
from jax.sharding import PartitionSpec as P

MESH = pl.DeviceIdType.MESH
F32 = jnp.float32
BF16 = jnp.bfloat16
DIRS = [(dr, dc) for dr in (-1, 0, 1) for dc in (-1, 0, 1) if (dr, dc) != (0, 0)]
SLOT = {d: s for s, d in enumerate(DIRS)}
MSG = 16
PARTS = 2
LOAD_ORDER = (0, 2, 5, 6, 3, 7, 8, 4, 9, 10, 1)


def mm(left, right, lhs_dim=1, rhs_dim=0):
    return lax.dot_general(
        left, right, (((lhs_dim,), (rhs_dim,)), ((), ())), preferred_element_type=F32
    )


def remote(src, dst, send, recv, target):
    copy = pltpu.make_async_remote_copy(
        src_ref=src, dst_ref=dst, send_sem=send, recv_sem=recv, device_id=target, device_id_type=MESH
    )
    copy.start()
    return copy


def placement(th, tw, row, rows, col, cols):
    base = th * tw
    at = {d: base + MSG * s for d, s in SLOT.items()}
    cells = (th + 2) * tw
    index = lax.broadcasted_iota(jnp.int32, (cells, 1), 0)
    r = index // tw - 1
    c = index % tw
    far = 1 << 16
    no_up = (row == 0).astype(jnp.int32) * far
    no_down = (row == rows - 1).astype(jnp.int32) * far
    no_left = (col == 0).astype(jnp.int32) * far
    no_right = (col == cols - 1).astype(jnp.int32) * far
    up, down = r < 0, r >= th
    lanes = lax.broadcasted_iota(jnp.int32, (cells, base + 8 * MSG), 1)
    result = []
    for shift in (-1, 0, 1):
        cc = c + shift
        src = jnp.where(
            up, at[(-1, 0)] + cc - no_up, jnp.where(down, at[(1, 0)] + cc - no_down, r * tw + cc)
        )
        if shift == -1:
            edge = jnp.where(
                up,
                at[(-1, -1)] + tw - 1 - no_up,
                jnp.where(down, at[(1, -1)] + tw - 1 - no_down, at[(0, -1)] + th + r),
            )
            src = jnp.where(cc < 0, edge - no_left, src)
        if shift == 1:
            edge = jnp.where(
                up, at[(-1, 1)] - no_up, jnp.where(down, at[(1, 1)] - no_down, at[(0, 1)] + r)
            )
            src = jnp.where(cc >= tw, edge - no_right, src)
        result.append(jnp.where(src == lanes, 1.0, 0.0).astype(BF16))
    return result


def kernel(rows, cols, th, tw, chunks, norm, *refs):
    hbm, refs = refs[:11], refs[11:]
    outs = refs[:4]
    local, refs = refs[4:15], refs[15:]
    x_ref, cot_ref, w1_ref, gw_ref, w3_ref, s1_ref, b1_ref, s2_ref, b2_ref, s3_ref, b3_ref = local
    cells1, cells2, side1, side2, place, dense, padded1, padded2 = refs[:8]
    slope1, slope2, back3, kgrad, x_turned = refs[8:13]
    gin_ref, g1_ref, gk_ref, g3_ref = refs[13:17]
    refs = refs[4:]
    units = [refs[13 + 4 * u : 17 + 4 * u] for u in range(2 + chunks)]
    (load_sem, out_sem, halo_send, halo_recv, rs_send, rs_recv, z_send, z_recv, ag_send, ag_recv) = refs[
        13 + 4 * (2 + chunks) :
    ]
    loads = []
    for index in LOAD_ORDER:
        copy = pltpu.make_async_copy(hbm[index], local[index], load_sem.at[index])
        copy.start()
        loads.append(copy)
    row, col = lax.axis_index("row"), lax.axis_index("col")
    x, z = col % 2, col // 2
    depth = cols // 2
    plane_n = rows * 2
    me = row * 2 + x
    n = th * tw
    hid = w1_ref.shape[1]
    width = gw_ref.shape[0] // 9

    halo_peers = [
        (lax.rem(row + dr + rows, rows), lax.rem(col + dc + cols, cols)) for dr, dc in DIRS
    ]
    plane_peers = []
    for dr in range(rows):
        for dx in range(2):
            if dr or dx:
                plane_peers.append((lax.rem(row + dr, rows), z * 2 + lax.rem(x + dx, 2)))
    z_peers = [(row, lax.rem(z + dz, depth) * 2 + x) for dz in range(1, depth)]

    def exists(dr, dc):
        ok = None
        for step, spot, count in ((dr, row, rows), (dc, col, cols)):
            if step:
                inside = spot > 0 if step < 0 else spot < count - 1
                ok = inside if ok is None else jnp.logical_and(ok, inside)
        return ok

    for cells in (cells1, cells2):
        cells[n:, :] = jnp.zeros((8 * MSG, hid), BF16)

    barrier = pltpu.get_barrier_semaphore()
    for peer in plane_peers + z_peers:
        pl.semaphore_signal(barrier, inc=1, device_id=peer, device_id_type=MESH)
    for (dr, dc), peer in zip(DIRS, halo_peers):

        @pl.when(exists(dr, dc))
        def _(peer=peer):
            pl.semaphore_signal(barrier, inc=1, device_id=peer, device_id_type=MESH)

    near_rows = 1 + (row > 0).astype(jnp.int32) + (row < rows - 1).astype(jnp.int32)
    near_cols = 1 + (col > 0).astype(jnp.int32) + (col < cols - 1).astype(jnp.int32)
    greeted = near_rows * near_cols - 1 + len(plane_peers) + len(z_peers)

    def border(which, cells, side, d, arriving):
        dr, dc = d
        src = side
        if dr == -1:
            src = cells.at[pl.ds(0, tw)]
        elif dr == 1:
            src = cells.at[pl.ds(n - tw, tw)]
        slot = SLOT[d] if arriving else SLOT[(-dr, -dc)]
        return pltpu.make_async_remote_copy(
            src_ref=src,
            dst_ref=cells.at[pl.ds(n + slot * MSG, MSG)],
            send_sem=halo_send.at[which, slot],
            recv_sem=halo_recv.at[which, slot],
            device_id=halo_peers[SLOT[d]],
            device_id_type=MESH,
        )

    def exchange(which, cells, side):
        for d in DIRS:

            @pl.when(exists(*d))
            def _(d=d):
                border(which, cells, side, d, False).start()

    def arrive(which, cells, side):
        for d in DIRS:

            @pl.when(exists(*d))
            def _(d=d):
                border(which, cells, side, d, True).wait_recv()

    def depart(which, cells, side):
        for d in DIRS:

            @pl.when(exists(*d))
            def _(d=d):
                border(which, cells, side, d, False).wait_send()

    def scatter(which, part, slots):
        piece = slots.shape[1]
        copies = []
        for k, peer in enumerate(plane_peers):
            theirs = peer[0] * 2 + peer[1] % 2
            copies.append(
                remote(
                    part.at[pl.ds(pl.multiple_of(theirs * piece, 16), piece)],
                    slots.at[k],
                    rs_send.at[which, k],
                    rs_recv.at[which, k],
                    peer,
                )
            )
        return copies

    def sum_plane(copies, part, slots, total):
        piece = slots.shape[1]
        for copy in copies:
            copy.wait_recv()
        value = part[pl.ds(pl.multiple_of(me * piece, 16), piece), :].astype(F32)
        for k in range(plane_n - 1):
            value = value + slots[k].astype(F32)
        total[z] = value.astype(BF16)

    def spread(which, total):
        return [
            remote(
                total.at[z], total.at[z], z_send.at[which, k], z_recv.at[which, k], peer
            )
            for k, peer in enumerate(z_peers)
        ]

    def sum_depth(copies, total, full):
        piece = total.shape[1]
        for copy in copies:
            copy.wait_recv()
        value = total[0].astype(F32)
        for k in range(1, depth):
            value = value + total[k].astype(F32)
        full[pl.ds(pl.multiple_of(me * piece, 16), piece), :] = value.astype(BF16)

    partner = (row + 1 - 2 * lax.rem(row, 2), col)
    across = [(dr, dx) for dr in range(0, rows, 2) for dx in range(2) if dr or dx]

    def gather(which, total, full):
        piece = total.shape[1]
        mine = full.at[pl.ds(pl.multiple_of(me * piece, 16), piece)]
        targets = [partner] + [
            (lax.rem(row + dr, rows), z * 2 + lax.rem(x + dx, 2)) for dr, dx in across
        ]
        return [
            remote(mine, mine, ag_send.at[which, k], ag_recv.at[which, k], peer)
            for k, peer in enumerate(targets)
        ]

    def relay(which, copies, full):
        piece = full.shape[0] // plane_n
        passed = []
        for k, (dr, dx) in enumerate(across):
            copies[1 + k].wait_recv()
            origin = lax.rem(row - dr + rows, rows) * 2 + lax.rem(x + dx, 2)
            held = full.at[pl.ds(pl.multiple_of(origin * piece, 16), piece)]
            slot = 1 + len(across) + k
            passed.append(
                remote(held, held, ag_send.at[which, slot], ag_recv.at[which, slot], partner)
            )
        return copies[:1] + passed

    pick_row = lax.broadcasted_iota(jnp.int32, (MSG, n), 0)
    pick_cell = lax.broadcasted_iota(jnp.int32, (MSG, n), 1)
    target = jnp.where(pick_row < th, pick_row * tw, (pick_row - th) * tw + tw - 1)
    pick = jnp.where(target == pick_cell, 1.0, 0.0).astype(BF16)

    for copy in loads[:4]:
        copy.wait()
    pre1 = mm(x_ref[...], w1_ref[...]) * s1_ref[...] + b1_ref[...]
    sig = jax.nn.sigmoid(pre1)
    act1 = (pre1 * sig).astype(BF16)
    cells1[0:n, :] = act1
    side1[...] = mm(pick, act1).astype(BF16)
    pl.semaphore_wait(barrier, greeted)
    exchange(0, cells1, side1)
    for copy in loads[4:]:
        copy.wait()

    slope1[...] = sig * (1.0 + pre1 * (1.0 - sig)) * s1_ref[...]
    for b, matrix in enumerate(placement(th, tw, row, rows, col, cols)):
        place[b] = matrix
    same = (
        lax.broadcasted_iota(jnp.int32, (hid, hid), 0) // width
        == lax.broadcasted_iota(jnp.int32, (hid, hid), 1) // width
    )
    keep = jnp.where(same, 1.0, 0.0)
    grouped = gw_ref[...].astype(F32)
    for tap in range(9):
        small = grouped[tap * width : (tap + 1) * width]
        tiled = jnp.broadcast_to(small[None], (hid // width, width, hid)).reshape(hid, hid)
        dense[tap] = (tiled * keep).astype(BF16)
    kgrad[...] = jnp.zeros_like(kgrad)

    x_turned[...] = x_ref[...].T

    arrive(0, cells1, side1)
    for b in range(3):
        padded1[b] = mm(place[b], cells1[...]).astype(BF16)

    total = None
    for a in range(3):
        for b in range(3):
            term = mm(padded1[b, a * tw : a * tw + n, :], dense[a * 3 + b])
            total = term if total is None else total + term
    pre2 = total * s2_ref[...] + b2_ref[...]
    sig = jax.nn.sigmoid(pre2)
    act2 = (pre2 * sig).astype(BF16)
    slope2[...] = sig * (1.0 + pre2 * (1.0 - sig)) * s2_ref[...]

    pre3 = mm(act2, w3_ref[...]) * s3_ref[...] + b3_ref[...] + x_ref[...].astype(F32)
    sig = jax.nn.sigmoid(pre3)
    back = cot_ref[...].astype(F32) * (sig * (1.0 + pre3 * (1.0 - sig)))
    back3[...] = back
    err3 = (back * s3_ref[...]).astype(BF16)

    err2 = (mm(err3, w3_ref[...], 1, 1) * slope2[...]).astype(BF16)
    cells2[0:n, :] = err2
    side2[...] = mm(pick, err2).astype(BF16)
    exchange(1, cells2, side2)

    started = []

    def unit(index, step, *extra):
        part, slots, total, full = units[index]
        if step == 0:
            copies = scatter(index, part, slots)
        elif step == 1:
            sum_plane(*extra, part, slots, total)
            copies = spread(index, total)
        else:
            sum_depth(*extra, total, full)
            copies = gather(index, total, full)
        started.extend(copies)
        return copies

    def forward(index, copies):
        result = relay(index, copies, units[index][3])
        started.extend(result[1:])
        return result

    third = mm(act2, err3, 0, 0)
    for half in range(third.shape[1] // hid):
        units[0][0][half * hid : (half + 1) * hid, :] = third[
            :, half * hid : (half + 1) * hid
        ].astype(BF16)
    t_now = unit(0, 0)
    for a in range(3):
        for b in range(3):
            tap = a * 3 + b
            square = mm(padded1[b, a * tw : a * tw + n, :], cells2[0:n, :], 0, 0) * keep
            kgrad[tap * width : (tap + 1) * width, :] = jnp.sum(
                square.reshape(hid // width, width, hid), axis=0
            )
    units[1][0][...] = kgrad[...].astype(BF16)
    k_now = unit(1, 0)

    arrive(1, cells2, side2)
    for b in range(3):
        padded2[b] = mm(place[b], cells2[...]).astype(BF16)
    total = None
    for a in range(3):
        for b in range(3):
            window = padded2[2 - b, (2 - a) * tw : (2 - a) * tw + n, :]
            term = mm(window, dense[a * 3 + b], 1, 1)
            total = term if total is None else total + term
    err1 = (total * slope1[...]).astype(BF16)
    span = hid // chunks
    f_now = []
    for chunk in range(chunks):
        units[2 + chunk][0][...] = mm(
            x_turned[...], err1[:, chunk * span : (chunk + 1) * span]
        ).astype(BF16)
        f_now.append(unit(2 + chunk, 0))

    t_now = unit(0, 1, t_now)
    k_now = unit(1, 1, k_now)
    for chunk in range(chunks):
        f_now[chunk] = unit(2 + chunk, 1, f_now[chunk])
    t_now = unit(0, 2, t_now)
    k_now = unit(1, 2, k_now)
    for chunk in range(chunks):
        f_now[chunk] = unit(2 + chunk, 2, f_now[chunk])
    t_now = forward(0, t_now)
    k_now = forward(1, k_now)
    gin_ref[...] = (back3[...] + mm(err1, w1_ref[...], 1, 1)).astype(BF16)
    stores = []

    def store(src, dst):
        copy = pltpu.make_async_copy(src, dst, out_sem.at[len(stores)])
        copy.start()
        stores.append(copy)

    store(gin_ref, outs[0])
    for chunk in range(chunks):
        f_now[chunk] = forward(2 + chunk, f_now[chunk])
    for copy in t_now:
        copy.wait_recv()
    for half in range(g3_ref.shape[1] // hid):
        g3_ref[:, half * hid : (half + 1) * hid] = (
            units[0][3][half * hid : (half + 1) * hid, :].astype(F32) * norm
        )
    store(g3_ref, outs[3])
    for copy in k_now:
        copy.wait_recv()
    gk_ref[...] = units[1][3][...].astype(F32)[: gk_ref.shape[0]] * norm
    store(gk_ref, outs[2])
    for chunk in range(chunks):
        for copy in f_now[chunk]:
            copy.wait_recv()
        lanes = pl.ds(chunk * span, span)
        g1_ref[:, lanes] = units[2 + chunk][3][...].astype(F32) * norm
        store(g1_ref.at[:, lanes], outs[1].at[:, lanes])
    depart(0, cells1, side1)
    depart(1, cells2, side2)
    for copy in started:
        copy.wait_send()
    for copy in stores:
        copy.wait()


def finish(*refs):
    sources, targets, held, sems = refs[:4], refs[4:8], refs[8:12], refs[12]
    reads, writes = [], []
    for k, (src, dst, hold) in enumerate(zip(sources, targets, held)):
        parts = PARTS if src.shape[0] % (16 * PARTS) == 0 else 1
        size = src.shape[0] // parts
        for part in range(parts):
            span = pl.ds(part * size, size)
            reads.append(pltpu.make_async_copy(src.at[span], hold.at[span], sems.at[0, k, part]))
            writes.append(pltpu.make_async_copy(hold.at[span], dst.at[span], sems.at[1, k, part]))
    for copy in reads:
        copy.start()
    for read, write in zip(reads, writes):
        read.wait()
        write.start()
    for copy in writes:
        copy.wait()


def body(mesh_rows, mesh_cols, inputs, cotangent, w1, gw, w3, s1, b1, s2, b2, s3, b3):
    th, tw, cin = inputs.shape
    hid = w1.shape[1]
    n = th * tw
    width = gw.shape[2]
    plane_n = mesh_rows * 2
    depth = mesh_cols // 2
    chunks = 2
    w_piece = cin // plane_n
    k_piece = -(-9 * width // plane_n)
    k_piece = -(-k_piece // 16) * 16
    hbm = pl.BlockSpec(memory_space=pltpu.HBM)
    out_shape = (
        jax.ShapeDtypeStruct((n, cin), BF16),
        jax.ShapeDtypeStruct((cin, hid), F32),
        jax.ShapeDtypeStruct((9 * width, hid), F32),
        jax.ShapeDtypeStruct((hid, cin), F32),
    )
    norm = 1.0 / math.sqrt(n * mesh_rows * mesh_cols)
    operands = (
        inputs.reshape(n, cin),
        cotangent.reshape(n, cin),
        w1,
        gw.reshape(9 * width, hid),
        w3,
        s1.reshape(1, -1),
        b1.reshape(1, -1),
        s2.reshape(1, -1),
        b2.reshape(1, -1),
        s3.reshape(1, -1),
        b3.reshape(1, -1),
    )
    cells = n + 8 * MSG
    padded = (3, (th + 2) * tw, hid)
    dma = pltpu.SemaphoreType.DMA
    unit_shapes = [(w_piece, hid), (k_piece, hid)] + [(w_piece, hid // chunks)] * chunks
    unit_scratch = []
    for piece, wide in unit_shapes:
        for shape in (
            (plane_n * piece, wide),
            (plane_n - 1, piece, wide),
            (depth, piece, wide),
            (plane_n * piece, wide),
        ):
            unit_scratch.append(pltpu.VMEM(shape, BF16))
    count = 2 + chunks
    results = pl.pallas_call(
        functools.partial(kernel, mesh_rows, mesh_cols, th, tw, chunks, norm),
        out_shape=out_shape,
        in_specs=[hbm] * 11,
        out_specs=(hbm,) * 4,
        scratch_shapes=[pltpu.VMEM(a.shape, a.dtype) for a in operands]
        + [
            pltpu.VMEM((cells, hid), BF16),
            pltpu.VMEM((cells, hid), BF16),
            pltpu.VMEM((MSG, hid), BF16),
            pltpu.VMEM((MSG, hid), BF16),
            pltpu.VMEM((3, (th + 2) * tw, cells), BF16),
            pltpu.VMEM((9, hid, hid), BF16),
            pltpu.VMEM(padded, BF16),
            pltpu.VMEM(padded, BF16),
            pltpu.VMEM((n, hid), F32),
            pltpu.VMEM((n, hid), F32),
            pltpu.VMEM((n, cin), F32),
            pltpu.VMEM((k_piece * plane_n, hid), F32),
            pltpu.VMEM((cin, n), BF16),
        ]
        + [pltpu.VMEM(a.shape, a.dtype) for a in out_shape]
        + unit_scratch
        + [
            dma((11,)),
            dma((3 + chunks,)),
            dma((2, 8)),
            dma((2, 8)),
            dma((count, plane_n - 1)),
            dma((count, plane_n - 1)),
            dma((count, depth - 1)),
            dma((count, depth - 1)),
            dma((count, plane_n - 1)),
            dma((count, plane_n - 1)),
        ],
        compiler_params=pltpu.CompilerParams(
            collective_id=0, has_side_effects=True, vmem_limit_bytes=60 << 20
        ),
    )(*operands)
    gin, g1, gk, g3 = pl.pallas_call(
        finish,
        out_shape=out_shape,
        in_specs=[hbm] * 4,
        out_specs=(hbm,) * 4,
        scratch_shapes=[pltpu.VMEM(a.shape, a.dtype) for a in out_shape] + [dma((2, 4, PARTS))],
        compiler_params=pltpu.CompilerParams(vmem_limit_bytes=60 << 20),
    )(*results)
    return gin.reshape(th, tw, cin), g1, gk.reshape(gw.shape), g3


def solution(mesh):
    tile = P("row", "col", None)
    return jax.shard_map(
        functools.partial(body, mesh.shape["row"], mesh.shape["col"]),
        mesh=mesh,
        in_specs=(tile, tile) + (P(),) * 9,
        out_specs=(tile, P(), P(), P()),
        check_vma=False,
    )
```
